32 devices in a mesh: cell: 8 (over z, y), stn: 4 (over x, core).
Axes of the slice: x: 2, y: 2, z: 4, core: 2. Of those that a mesh axis runs over, the one named last changes fastest.
Arguments:
- cell_points: float32 [3, 8192], P(None, 'cell'), may hold values from 0 to 1
- magnetization: float32 [3, 8192], P(None, 'cell'), may hold values from -6 to 6
- cell_level: int32 [8192], P('cell'), may hold values from 0 to 2
- suscept: float32 [8192], P('cell'), may hold values from 0.2 to 2
- inducing: float32 [3], replicated, may hold values from -4 to 4
- stations: float32 [3, 4096], P(None, 'stn'), may hold values from 0 to 2, as said below
Outputs:
- updated: float32 [3, 8192], P(None, ('cell', 'stn'))
- predictions: float32 [4096], P(('stn', 'cell'))
The draws below stay inside these ranges and needn't reach their ends.
Inputs may be any that keep to these rules, and one draw needn't show every extreme that they name: `stations`: the first two coordinates lie in the unit square; the third is 1 plus 0.5 to 2 times 8192 ** (-1/3).
All inputs are finite; a program needn't handle non-finite values.
Results may differ from the reference program's by a relative error of at most 0.0003.
Values sent between devices are 32-bit elements; how exact they have to be, the bound alone decides.
A program may use at most 64 MiB of HBM per device.

```python
import math
import jax
import jax.numpy as jnp
from jax import lax

NC = 8192
NS = 4096


def cell_centres(key):
    return jax.random.uniform(jax.random.fold_in(key, 11), (3, NC), jnp.float32, 0.0, 1.0)


def draw_cell_points(key, part):
    return cell_centres(key)


def draw_magnetization(key, part):
    centres = cell_centres(key)
    keys = jax.random.split(jax.random.fold_in(key, 29), 7)
    height = jax.random.uniform(keys[0], (), jnp.float32, -1.0, 1.0)
    turn = jax.random.uniform(keys[1], (), jnp.float32, -math.pi, math.pi)
    across = jnp.sqrt(1.0 - height * height)
    direction = jnp.stack([across * jnp.cos(turn), across * jnp.sin(turn), height], 0)
    frequency = jax.random.uniform(keys[2], (3, 4, 3), jnp.float32, 0.5, 2.0)
    phase = jax.random.uniform(keys[3], (3, 4), jnp.float32, -math.pi, math.pi)
    amplitude = jax.random.uniform(keys[4], (3, 4), jnp.float32, 0.2, 0.5)
    argument = frequency[:, :, 0, None] * centres[0][None, None, :]
    argument = argument + frequency[:, :, 1, None] * centres[1][None, None, :]
    argument = argument + frequency[:, :, 2, None] * centres[2][None, None, :]
    waves = amplitude[:, :, None] * jnp.cos(2.0 * math.pi * argument + phase[:, :, None])
    smooth = waves[:, 0] + waves[:, 1] + waves[:, 2] + waves[:, 3]
    strength = jax.random.uniform(keys[5], (), jnp.float32, 1.0, 3.0)
    noise = 0.4 * jax.random.normal(keys[6], (3, NC), jnp.float32)
    result = strength * direction[:, None] + smooth + noise
    return jnp.clip(result, -6.0, 6.0)


def draw_stations(key, part):
    first_key, second_key = jax.random.split(jax.random.fold_in(key, 17))
    spacing = float(NC) ** (-1.0 / 3.0)
    flat = jax.random.uniform(first_key, (2, NS), jnp.float32, 0.0, 1.0)
    height = 1.0 + spacing * jax.random.uniform(second_key, (1, NS), jnp.float32, 0.5, 2.0)
    return jnp.concatenate([flat, height], 0)


def with_ends(array, key, low, largest):
    shape = array.shape
    index_at = [jax.random.randint(jax.random.fold_in(key, axis), (), 0, shape[axis]) for axis in range(len(shape))]
    array = array.at[tuple(index_at)].set(low)
    longest = shape.index(max(shape))
    index_at[longest] = (index_at[longest] + 1) % shape[longest]
    return array.at[tuple(index_at)].set(largest)


def shard_levels(stream_key, extent, cuts, smallest, largest):
    def one(axis_at, parts):
        draws = jax.random.uniform(jax.random.fold_in(jax.random.fold_in(stream_key, 6), axis_at), (parts,), jnp.float32, smallest / len(cuts), largest / len(cuts))
        return jnp.repeat(jnp.exp(draws), extent[axis_at] // parts).reshape((-1,) + (1,) * (len(extent) - axis_at - 1))

    loudness = one(*cuts[0])
    for cut in cuts[1:]:
        loudness = loudness * one(*cut)
    return loudness


def normal_values(stream_key, shape, spread, most, dtype=jnp.bfloat16):
    values = spread * jax.random.normal(stream_key, shape, jnp.float32)
    return jnp.clip(values, min=-most, max=most).astype(dtype)


def setup_inputs(seed: int = 0) -> dict:
    splits = jax.random.split(jax.random.key(seed), 7)
    cell_points = draw_cell_points(jax.random.fold_in(splits[6], 71), 0)
    magnetization = draw_magnetization(jax.random.fold_in(splits[6], 71), 0)
    cell_level = with_ends(jax.random.randint(splits[2], (NC,), 0, 3), jax.random.fold_in(splits[2], 1), 0, 2).astype(jnp.int32)
    suscept = jnp.clip(jnp.exp(math.log(2.0) - 2.3025851 * jax.random.uniform(splits[3], (NC,), jnp.float32) ** shard_levels(splits[3], (NC,), ((0, 8),), -0.2, 0.2)), 0.2, 2.0)
    inducing = normal_values(splits[4], (3,), 1.0, 4.0, jnp.float32)
    stations = draw_stations(jax.random.fold_in(splits[6], 71), 0)
    return {"cell_points": cell_points, "magnetization": magnetization, "cell_level": cell_level, "suscept": suscept, "inducing": inducing, "stations": stations}


INV_FOUR_PI = 0.25 / math.pi

def block_width(targets, sources):
    ceiling = max(256, (1 << 20) // targets)
    ceiling = 1 << ceiling.bit_length() - 1
    return math.gcd(sources, ceiling)

def pair_field(points, source_piece):
    delta_x = points[0][:, None] - source_piece[0][None, :]
    delta_y = points[1][:, None] - source_piece[1][None, :]
    delta_z = points[2][:, None] - source_piece[2][None, :]
    soften = source_piece[6][None, :]
    radius_sq = delta_x * delta_x + delta_y * delta_y + delta_z * delta_z + soften * soften
    inverse = lax.rsqrt(radius_sq)
    inverse_sq = inverse * inverse
    weight = INV_FOUR_PI * soften * soften * soften * inverse_sq * inverse
    projection = 3.0 * (delta_x * source_piece[3][None, :] + delta_y * source_piece[4][None, :] + delta_z * source_piece[5][None, :]) * inverse_sq
    field_x = lax.optimization_barrier(jnp.sum(weight * (projection * delta_x - source_piece[3][None, :]), axis=1))
    field_y = lax.optimization_barrier(jnp.sum(weight * (projection * delta_y - source_piece[4][None, :]), axis=1))
    field_z = lax.optimization_barrier(jnp.sum(weight * (projection * delta_z - source_piece[5][None, :]), axis=1))
    return jnp.stack([field_x, field_y, field_z], 0)

def source_field(points, sources):
    number = sources.shape[1]
    blockw = block_width(points.shape[1], number)
    groups = sources.reshape(7, number // blockw, blockw).transpose(1, 0, 2)

    def advance(summed, source_piece):
        return (summed + pair_field(points, source_piece), None)
    result, unused = lax.scan(advance, jnp.zeros((3, points.shape[1]), jnp.float32), groups)
    return result

def fields_at(points, sources):
    number = points.shape[1]
    blockw = math.gcd(number, 512)
    groups = points.reshape(3, number // blockw, blockw).transpose(1, 0, 2)

    def target_block(group):
        return source_field(group, sources)
    result = lax.map(target_block, groups)
    return result.transpose(1, 0, 2).reshape(3, number)

def reference(cell_points, magnetization, cell_level, suscept, inducing, stations):
    spacing = float(NC) ** (-1.0 / 3.0)
    size_h = spacing * jnp.power(0.5, cell_level.astype(jnp.float32))
    sources = jnp.concatenate([cell_points, magnetization, size_h[None, :]], 0)
    demag = fields_at(cell_points, sources)
    updated = suscept[None, :] * (inducing[:, None] + demag)
    moved = jnp.concatenate([cell_points, updated, size_h[None, :]], 0)
    field = fields_at(stations, moved)
    predictions = lax.optimization_barrier(jnp.sum(inducing[:, None] * field, axis=0))
    return (updated, predictions)
```

```python
import functools
import math

import jax
import jax.numpy as jnp
from jax import lax
from jax.experimental import pallas as pl
from jax.experimental.pallas import tpu as pltpu
from jax.sharding import PartitionSpec as P

INV_FOUR_PI = 0.25 / math.pi
MESH = pl.DeviceIdType.MESH
LANES = 128
ROWS = 32


def partner(me, k, n):
    out, bit = 0, 1
    while bit < n:
        out = out + bit * (((me // bit) % 2 + (k // bit) % 2) % 2)
        bit *= 2
    return out


def lane_sums(values):
    ones = jnp.ones((8, LANES), jnp.float32)
    return lax.dot_general(
        ones,
        values,
        (((1,), (1,)), ((), ())),
        precision=lax.Precision.HIGHEST,
        preferred_element_type=jnp.float32,
    )


def kernel(
    nc, ns, cp, mg, lv, su, ind, st, upd, pred,
    pack, gath, tgt, acc, xi, mag, stb, racc, pbuf, rbuf,
    send1, recv1, send2, recv2, send3, recv3,
):
    block = cp.shape[1]
    owned = block // ns
    stations = st.shape[1]
    spacing = float(block * nc) ** (-1.0 / 3.0)
    c_me = lax.axis_index("cell")
    s_me = lax.axis_index("stn")

    barrier = pltpu.get_barrier_semaphore()

    @pl.loop(1, nc)
    def _(k):
        pl.semaphore_signal(barrier, inc=1, device_id={"cell": partner(c_me, k, nc)}, device_id_type=MESH)

    @pl.loop(1, ns)
    def _(k):
        pl.semaphore_signal(barrier, inc=1, device_id={"stn": partner(s_me, k, ns)}, device_id_type=MESH)

    level = lv[...]
    size_h = spacing * jnp.where(level == 0, 1.0, jnp.where(level == 1, 0.5, 0.25))
    strength = INV_FOUR_PI * size_h * size_h * size_h
    pack[0:3, :] = cp[...]
    pack[3:6, :] = mg[...] * strength
    pack[6:7, :] = size_h * size_h
    pack[7:8, :] = strength

    pl.semaphore_wait(barrier, nc - 1 + ns - 1)

    def copy1(k):
        return pltpu.make_async_remote_copy(
            src_ref=pack, dst_ref=gath.at[k - 1], send_sem=send1.at[k - 1], recv_sem=recv1.at[k - 1],
            device_id={"cell": partner(c_me, k, nc)}, device_id_type=MESH,
        )

    @pl.loop(1, nc)
    def _(k):
        copy1(k).start()

    offset = s_me * owned
    ix, iy, iz = ind[0], ind[1], ind[2]
    for d in range(3):
        for t in range(owned // LANES):
            row = cp[d : d + 1, pl.ds(pl.multiple_of(offset + t * LANES, LANES), LANES)]
            tgt[d, t * LANES : (t + 1) * LANES, :] = jnp.broadcast_to(row, (LANES, LANES)).T
    acc[...] = jnp.zeros_like(acc)

    def sweep(src):
        @pl.loop(0, owned // ROWS)
        def _(g):
            rows = pl.ds(pl.multiple_of(g * ROWS, ROWS), ROWS)
            px, py, pz = tgt[0, rows, :], tgt[1, rows, :], tgt[2, rows, :]

            def chunks(start, count, sums):
                ax, ay, az = sums
                for j in range(count):
                    at = pl.ds(start + j * LANES, LANES)

                    def row(r):
                        return jnp.broadcast_to(src[r : r + 1, at], (ROWS, LANES))

                    dx, dy, dz = px - row(0), py - row(1), pz - row(2)
                    mx, my, mz = row(3), row(4), row(5)
                    inv = lax.rsqrt(dx * dx + dy * dy + dz * dz + row(6))
                    inv2 = inv * inv
                    inv3 = inv2 * inv
                    along = 3.0 * (dx * mx + dy * my + dz * mz) * inv2
                    ax = ax + inv3 * (along * dx - mx)
                    ay = ay + inv3 * (along * dy - my)
                    az = az + inv3 * (along * dz - mz)
                return ax, ay, az

            sums = (acc[0, rows, :], acc[1, rows, :], acc[2, rows, :])
            step = 8
            total = block // (LANES * step)
            if total == 1:
                sums = chunks(0, step, sums)
            else:
                sums = lax.fori_loop(
                    0, total, lambda i, s: chunks(pl.multiple_of(i * step * LANES, LANES), step, s), sums
                )
            acc[0, rows, :], acc[1, rows, :], acc[2, rows, :] = sums

    sweep(pack)

    @pl.loop(0, stations // LANES)
    def _(t):
        at = pl.ds(pl.multiple_of(t * LANES, LANES), LANES)
        x, y, z = [jnp.broadcast_to(st[d : d + 1, at], (LANES, LANES)).T for d in range(3)]
        stb[0, at, :] = x
        stb[1, at, :] = y
        stb[2, at, :] = z
        stb[3, at, :] = x * ix + y * iy + z * iz

    xi[...] = cp[0:1, :] * ix + cp[1:2, :] * iy + cp[2:3, :] * iz
    racc[...] = jnp.zeros_like(racc)

    @pl.loop(1, nc)
    def _(k):
        copy1(k).wait_recv()
        sweep(gath.at[k - 1])

    own = pl.ds(pl.multiple_of(offset, LANES), owned)
    gain = su[0:1, own]
    c_own = pack[7:8, own]
    new = [gain * (i + lane_sums(acc[d])[0:1]) for d, i in enumerate((ix, iy, iz))]
    for d in range(3):
        mag[s_me, d : d + 1, :] = 3.0 * c_own * new[d]
    mag[s_me, 3:4, :] = c_own * (new[0] * ix + new[1] * iy + new[2] * iz)

    def copy2(k):
        return pltpu.make_async_remote_copy(
            src_ref=mag.at[s_me], dst_ref=mag.at[s_me], send_sem=send2.at[k - 1], recv_sem=recv2.at[k - 1],
            device_id={"stn": partner(s_me, k, ns)}, device_id_type=MESH,
        )

    @pl.loop(1, ns)
    def _(k):
        copy2(k).start()

    for d in range(3):
        upd[d : d + 1, :] = new[d]

    def predict(k):
        who = partner(s_me, k, ns)

        @pl.loop(0, stations // ROWS)
        def _(g):
            rows = pl.ds(pl.multiple_of(g * ROWS, ROWS), ROWS)
            px, py, pz, pi = stb[0, rows, :], stb[1, rows, :], stb[2, rows, :], stb[3, rows, :]
            total = racc[rows, :]
            for j in range(owned // LANES):
                at = pl.ds(pl.multiple_of(who * owned + j * LANES, LANES), LANES)
                here = slice(j * LANES, (j + 1) * LANES)

                def spread(row):
                    return jnp.broadcast_to(row, (ROWS, LANES))

                dx, dy, dz = [p - spread(pack[d : d + 1, at]) for d, p in enumerate((px, py, pz))]
                mx, my, mz = [spread(mag[who, d : d + 1, here]) for d in range(3)]
                inv = lax.rsqrt(dx * dx + dy * dy + dz * dz + spread(pack[6:7, at]))
                inv2 = inv * inv
                both = (dx * mx + dy * my + dz * mz) * (pi - spread(xi[0:1, at]))
                total = total + (both * inv2 - spread(mag[who, 3:4, here])) * (inv2 * inv)
            racc[rows, :] = total

    predict(0)

    @pl.loop(1, ns)
    def _(k):
        copy2(k).wait_recv()
        predict(k)

    summed = lane_sums(racc[...])
    for c in range(nc):
        pbuf[c] = summed[:, c * LANES : (c + 1) * LANES]

    def copy3(k):
        who = partner(c_me, k, nc)
        return pltpu.make_async_remote_copy(
            src_ref=pbuf.at[who], dst_ref=rbuf.at[k - 1], send_sem=send3.at[k - 1], recv_sem=recv3.at[k - 1],
            device_id={"cell": who}, device_id_type=MESH,
        )

    @pl.loop(1, nc)
    def _(k):
        copy3(k).start()

    @pl.loop(1, nc)
    def _(k):
        copy3(k).wait_recv()

    result = pbuf[c_me]
    for k in range(nc - 1):
        result = result + rbuf[k]
    pred[...] = result[0:1]

    @pl.loop(1, nc)
    def _(k):
        copy1(k).wait_send()
        copy3(k).wait_send()

    @pl.loop(1, ns)
    def _(k):
        copy2(k).wait_send()


def shards(cell_points, magnetization, cell_level, suscept, inducing, stations):
    nc = lax.axis_size("cell")
    ns = lax.axis_size("stn")
    block = cell_points.shape[1]
    owned = block // ns
    targets = stations.shape[1]
    share = targets // nc
    f32 = jnp.float32
    vmem = pl.BlockSpec(memory_space=pltpu.VMEM)
    smem = pl.BlockSpec(memory_space=pltpu.SMEM)
    dma = pltpu.SemaphoreType.DMA
    updated, predictions = pl.pallas_call(
        functools.partial(kernel, nc, ns),
        out_shape=(jax.ShapeDtypeStruct((3, owned), f32), jax.ShapeDtypeStruct((1, share), f32)),
        in_specs=[vmem, vmem, vmem, vmem, smem, vmem],
        out_specs=(vmem, vmem),
        scratch_shapes=[
            pltpu.VMEM((8, block), f32),
            pltpu.VMEM((nc - 1, 8, block), f32),
            pltpu.VMEM((3, owned, LANES), f32),
            pltpu.VMEM((3, owned, LANES), f32),
            pltpu.VMEM((1, block), f32),
            pltpu.VMEM((ns, 8, owned), f32),
            pltpu.VMEM((4, targets, LANES), f32),
            pltpu.VMEM((targets, LANES), f32),
            pltpu.VMEM((nc, 8, share), f32),
            pltpu.VMEM((nc - 1, 8, share), f32),
            dma((nc - 1,)),
            dma((nc - 1,)),
            dma((ns - 1,)),
            dma((ns - 1,)),
            dma((nc - 1,)),
            dma((nc - 1,)),
        ],
        compiler_params=pltpu.CompilerParams(
            collective_id=0, has_side_effects=True, vmem_limit_bytes=40 * 1024 * 1024
        ),
    )(
        cell_points,
        magnetization,
        cell_level.reshape(1, block),
        suscept.reshape(1, block),
        inducing,
        stations,
    )
    return updated, predictions.reshape(share)


def solution(mesh):
    placed = (P(None, "cell"), P(None, "cell"), P("cell"), P("cell"), P(), P(None, "stn"))
    return jax.shard_map(
        shards,
        mesh=mesh,
        in_specs=placed,
        out_specs=(P(None, ("cell", "stn")), P(("stn", "cell"))),
        check_vma=False,
    )
```

```python
import functools
import math

import jax
import jax.numpy as jnp
from jax import lax
from jax.experimental import pallas as pl
from jax.experimental.pallas import tpu as pltpu
from jax.sharding import PartitionSpec as P

INV_FOUR_PI = 0.25 / math.pi
MESH = pl.DeviceIdType.MESH
LANES = 128
ROWS = 32


def partner(me, k, n):
    out, bit = 0, 1
    while bit < n:
        out = out + bit * (((me // bit) % 2 + (k // bit) % 2) % 2)
        bit *= 2
    return out


def lane_sums(values):
    ones = jnp.ones((8, LANES), jnp.float32)
    return lax.dot_general(
        ones,
        values,
        (((1,), (1,)), ((), ())),
        precision=lax.Precision.HIGHEST,
        preferred_element_type=jnp.float32,
    )


def kernel(
    nc, ns, cp_hbm, mg_hbm, lv_hbm, su_hbm, ind_hbm, st_hbm, upd, pred,
    cp, mg, lv, su, ind, st, cvol, gath, tgt, acc, mag, stb, racc,
    send1, recv1, send2, recv2, loaded,
):
    loads = [
        pltpu.make_async_copy(src, dst, loaded.at[i])
        for i, (src, dst) in enumerate(
            ((lv_hbm, lv), (mg_hbm, mg), (cp_hbm, cp), (ind_hbm, ind), (st_hbm, st), (su_hbm, su))
        )
    ]
    for load in loads:
        load.start()
    block = cp.shape[1]
    owned = block // ns
    share = st.shape[1] // nc
    spacing = float(block * nc) ** (-1.0 / 3.0)
    c_me = lax.axis_index("cell")
    s_me = lax.axis_index("stn")

    barrier = pltpu.get_barrier_semaphore()

    @pl.loop(1, nc)
    def _(k):
        pl.semaphore_signal(barrier, inc=1, device_id={"cell": partner(c_me, k, nc)}, device_id_type=MESH)

    @pl.loop(1, ns)
    def _(k):
        pl.semaphore_signal(barrier, inc=1, device_id={"stn": partner(s_me, k, ns)}, device_id_type=MESH)

    for load in loads[:4]:
        load.wait()
    ix, iy, iz = ind[0], ind[1], ind[2]
    level = lv[...]
    size_h = spacing * jnp.where(level == 0, 1.0, jnp.where(level == 1, 0.5, 0.25))
    strength = INV_FOUR_PI * size_h * size_h * size_h
    pack = gath.at[0]
    pack[0:3, :] = cp[...]
    pack[3:6, :] = mg[...] * strength
    pack[6:7, :] = size_h * size_h
    pack[7:8, :] = cp[0:1, :] * ix + cp[1:2, :] * iy + cp[2:3, :] * iz
    cvol[...] = strength

    pl.semaphore_wait(barrier, nc - 1 + ns - 1)

    def copy1(k):
        return pltpu.make_async_remote_copy(
            src_ref=gath.at[0], dst_ref=gath.at[k], send_sem=send1.at[k], recv_sem=recv1.at[k],
            device_id={"cell": partner(c_me, k, nc)}, device_id_type=MESH,
        )

    @pl.loop(1, nc)
    def _(k):
        copy1(k).start()

    offset = s_me * owned
    own = pl.ds(pl.multiple_of(offset, LANES), owned)
    for d in range(3):
        for t in range(owned // LANES):
            row = cp[d : d + 1, pl.ds(pl.multiple_of(offset + t * LANES, LANES), LANES)]
            tgt[d, t * LANES : (t + 1) * LANES, :] = jnp.broadcast_to(row, (LANES, LANES)).T
    acc[...] = jnp.zeros_like(acc)

    for load in loads[4:]:
        load.wait()
    mine = pl.ds(pl.multiple_of(c_me * share, LANES), share)
    place = [jnp.broadcast_to(st[d : d + 1, mine], (LANES, share)).T for d in range(3)]
    for d in range(3):
        stb[d] = place[d]
    stb[3] = place[0] * ix + place[1] * iy + place[2] * iz
    racc[...] = jnp.zeros_like(racc)

    def sweep(src):
        @pl.loop(0, owned // ROWS)
        def _(g):
            rows = pl.ds(pl.multiple_of(g * ROWS, ROWS), ROWS)
            px, py, pz = tgt[0, rows, :], tgt[1, rows, :], tgt[2, rows, :]

            def chunks(start, count, sums):
                ax, ay, az = sums
                for j in range(count):
                    at = pl.ds(start + j * LANES, LANES)

                    def row(r):
                        return jnp.broadcast_to(src[r : r + 1, at], (ROWS, LANES))

                    dx, dy, dz = px - row(0), py - row(1), pz - row(2)
                    mx, my, mz = row(3), row(4), row(5)
                    inv = lax.rsqrt(dx * dx + dy * dy + dz * dz + row(6))
                    inv2 = inv * inv
                    inv3 = inv2 * inv
                    along = 3.0 * (dx * mx + dy * my + dz * mz) * inv2
                    ax = ax + inv3 * (along * dx - mx)
                    ay = ay + inv3 * (along * dy - my)
                    az = az + inv3 * (along * dz - mz)
                return ax, ay, az

            sums = (acc[0, rows, :], acc[1, rows, :], acc[2, rows, :])
            step = 8
            total = block // (LANES * step)
            if total == 1:
                sums = chunks(0, step, sums)
            else:
                sums = lax.fori_loop(
                    0, total, lambda i, s: chunks(pl.multiple_of(i * step * LANES, LANES), step, s), sums
                )
            acc[0, rows, :], acc[1, rows, :], acc[2, rows, :] = sums

    sweep(pack)

    @pl.loop(1, nc)
    def _(k):
        copy1(k).wait_recv()
        sweep(gath.at[k])

    gain = su[0:1, own]
    c_own = cvol[0:1, own]
    me = c_me * ns + s_me
    new = [gain * (i + lane_sums(acc[d])[0:1]) for d, i in enumerate((ix, iy, iz))]
    for d in range(3):
        mag[me, d : d + 1, :] = 3.0 * c_own * new[d]
    mag[me, 3:4, :] = c_own * (new[0] * ix + new[1] * iy + new[2] * iz)

    def copy2(k, slot):
        kc, ks = k // ns, k % ns
        return pltpu.make_async_remote_copy(
            src_ref=mag.at[me], dst_ref=mag.at[slot], send_sem=send2.at[k], recv_sem=recv2.at[slot],
            device_id={"cell": partner(c_me, kc, nc), "stn": partner(s_me, ks, ns)}, device_id_type=MESH,
        )

    @pl.loop(1, nc * ns)
    def _(k):
        copy2(k, me).start()

    for d in range(3):
        upd[d : d + 1, :] = new[d]

    def predict(kc, s_who, who):
        for j in range(owned // LANES):
            at = pl.ds(pl.multiple_of(s_who * owned + j * LANES, LANES), LANES)
            here = slice(j * LANES, (j + 1) * LANES)

            def spread(row):
                return jnp.broadcast_to(row, (share, LANES))

            dx, dy, dz = [stb[d] - spread(gath[kc, d : d + 1, at]) for d in range(3)]
            mx, my, mz = [spread(mag[who, d : d + 1, here]) for d in range(3)]
            inv = lax.rsqrt(dx * dx + dy * dy + dz * dz + spread(gath[kc, 6:7, at]))
            inv2 = inv * inv
            both = (dx * mx + dy * my + dz * mz) * (stb[3] - spread(gath[kc, 7:8, at]))
            racc[...] += (both * inv2 - spread(mag[who, 3:4, here])) * (inv2 * inv)

    predict(0, s_me, me)

    @pl.loop(1, nc * ns)
    def _(k):
        kc, ks = k // ns, k % ns
        s_who = partner(s_me, ks, ns)
        who = partner(c_me, kc, nc) * ns + s_who
        copy2(k, who).wait_recv()
        predict(kc, s_who, who)

    pred[...] = lane_sums(racc[...])[0:1]

    @pl.loop(1, nc)
    def _(k):
        copy1(k).wait_send()

    @pl.loop(1, nc * ns)
    def _(k):
        copy2(k, me).wait_send()


def shards(cell_points, magnetization, cell_level, suscept, inducing, stations):
    nc = lax.axis_size("cell")
    ns = lax.axis_size("stn")
    block = cell_points.shape[1]
    owned = block // ns
    targets = stations.shape[1]
    share = targets // nc
    f32 = jnp.float32
    vmem = pl.BlockSpec(memory_space=pltpu.VMEM)
    hbm = pl.BlockSpec(memory_space=pltpu.HBM)
    dma = pltpu.SemaphoreType.DMA
    updated, predictions = pl.pallas_call(
        functools.partial(kernel, nc, ns),
        out_shape=(jax.ShapeDtypeStruct((3, owned), f32), jax.ShapeDtypeStruct((1, share), f32)),
        in_specs=[hbm] * 6,
        out_specs=(vmem, vmem),
        scratch_shapes=[
            pltpu.VMEM((3, block), f32),
            pltpu.VMEM((3, block), f32),
            pltpu.VMEM((1, block), jnp.int32),
            pltpu.VMEM((1, block), f32),
            pltpu.SMEM((3,), f32),
            pltpu.VMEM((3, targets), f32),
            pltpu.VMEM((1, block), f32),
            pltpu.VMEM((nc, 8, block), f32),
            pltpu.VMEM((3, owned, LANES), f32),
            pltpu.VMEM((3, owned, LANES), f32),
            pltpu.VMEM((nc * ns, 4, owned), f32),
            pltpu.VMEM((4, share, LANES), f32),
            pltpu.VMEM((share, LANES), f32),
            dma((nc,)),
            dma((nc,)),
            dma((nc * ns,)),
            dma((nc * ns,)),
            dma((6,)),
        ],
        compiler_params=pltpu.CompilerParams(
            collective_id=0, has_side_effects=True, vmem_limit_bytes=60 * 1024 * 1024
        ),
    )(
        cell_points,
        magnetization,
        cell_level.reshape(1, block),
        suscept.reshape(1, block),
        inducing,
        stations,
    )
    return updated, predictions.reshape(share)


def solution(mesh):
    placed = (P(None, "cell"), P(None, "cell"), P("cell"), P("cell"), P(), P(None, "stn"))
    return jax.shard_map(
        shards,
        mesh=mesh,
        in_specs=placed,
        out_specs=(P(None, ("cell", "stn")), P(("stn", "cell"))),
        check_vma=False,
    )
```

```python
import functools
import math

import jax
import jax.numpy as jnp
from jax import lax
from jax.experimental import pallas as pl
from jax.experimental.pallas import tpu as pltpu
from jax.sharding import PartitionSpec as P

INV_FOUR_PI = 0.25 / math.pi
MESH = pl.DeviceIdType.MESH
LANES = 128
ROWS = 32


def partner(me, k, n):
    out, bit = 0, 1
    while bit < n:
        out = out + bit * (((me // bit) % 2 + (k // bit) % 2) % 2)
        bit *= 2
    return out


def lane_sums(values):
    ones = jnp.ones((8, LANES), jnp.float32)
    return lax.dot_general(
        ones,
        values,
        (((1,), (1,)), ((), ())),
        precision=lax.Precision.HIGHEST,
        preferred_element_type=jnp.float32,
    )


def kernel(
    nc, ns, cp_hbm, mg_hbm, lv_hbm, su_hbm, ind_hbm, st_hbm, upd, pred,
    cp, mg, lv, su, ind, st, cvol, gath, tgt, acc, mag, stb, racc, geo, third,
    send1, recv1, send2, recv2, loaded,
):
    loads = [
        pltpu.make_async_copy(src, dst, loaded.at[i])
        for i, (src, dst) in enumerate(
            ((lv_hbm, lv), (mg_hbm, mg), (cp_hbm, cp), (ind_hbm, ind), (st_hbm, st), (su_hbm, su))
        )
    ]
    for load in loads:
        load.start()
    block = cp.shape[1]
    owned = block // ns
    share = st.shape[1] // nc
    spacing = float(block * nc) ** (-1.0 / 3.0)
    c_me = lax.axis_index("cell")
    s_me = lax.axis_index("stn")

    barrier = pltpu.get_barrier_semaphore()

    @pl.loop(1, nc)
    def _(k):
        pl.semaphore_signal(barrier, inc=1, device_id={"cell": partner(c_me, k, nc)}, device_id_type=MESH)

    @pl.loop(1, ns)
    def _(k):
        pl.semaphore_signal(barrier, inc=1, device_id={"stn": partner(s_me, k, ns)}, device_id_type=MESH)

    for load in loads[:4]:
        load.wait()
    ix, iy, iz = ind[0], ind[1], ind[2]
    level = lv[...]
    size_h = spacing * jnp.where(level == 0, 1.0, jnp.where(level == 1, 0.5, 0.25))
    strength = INV_FOUR_PI * size_h * size_h * size_h
    pack = gath.at[0]
    pack[0:3, :] = cp[...]
    pack[3:6, :] = mg[...] * strength
    pack[6:7, :] = size_h * size_h
    pack[7:8, :] = cp[0:1, :] * ix + cp[1:2, :] * iy + cp[2:3, :] * iz
    cvol[...] = strength

    pl.semaphore_wait(barrier, nc - 1 + ns - 1)

    def copy1(k):
        return pltpu.make_async_remote_copy(
            src_ref=gath.at[0], dst_ref=gath.at[k], send_sem=send1.at[k], recv_sem=recv1.at[k],
            device_id={"cell": partner(c_me, k, nc)}, device_id_type=MESH,
        )

    @pl.loop(1, nc)
    def _(k):
        copy1(k).start()

    offset = s_me * owned
    own = pl.ds(pl.multiple_of(offset, LANES), owned)
    for d in range(3):
        for t in range(owned // LANES):
            row = cp[d : d + 1, pl.ds(pl.multiple_of(offset + t * LANES, LANES), LANES)]
            tgt[d, t * LANES : (t + 1) * LANES, :] = jnp.broadcast_to(row, (LANES, LANES)).T
    acc[...] = jnp.zeros_like(acc)

    for load in loads[4:]:
        load.wait()
    mine = pl.ds(pl.multiple_of(c_me * share, LANES), share)
    place = [jnp.broadcast_to(st[d : d + 1, mine], (LANES, share)).T for d in range(3)]
    for d in range(3):
        stb[d] = place[d]
    stb[3] = place[0] * ix + place[1] * iy + place[2] * iz
    racc[...] = jnp.zeros_like(racc)

    def sweep(src):
        third[...] = src[3:6, :] * (1.0 / 3.0)

        @pl.loop(0, owned // ROWS)
        def _(g):
            rows = pl.ds(pl.multiple_of(g * ROWS, ROWS), ROWS)
            px, py, pz = tgt[0, rows, :], tgt[1, rows, :], tgt[2, rows, :]

            def chunks(start, count, sums):
                ax, ay, az = sums
                for j in range(count):
                    at = pl.ds(start + j * LANES, LANES)

                    def row(r):
                        return jnp.broadcast_to(src[r : r + 1, at], (ROWS, LANES))

                    dx, dy, dz = px - row(0), py - row(1), pz - row(2)
                    mx, my, mz = row(3), row(4), row(5)
                    inv = lax.rsqrt(dx * dx + dy * dy + dz * dz + row(6))
                    inv2 = inv * inv
                    inv3 = inv2 * inv
                    along = (dx * mx + dy * my + dz * mz) * inv2
                    tx, ty, tz = [
                        jnp.broadcast_to(third[d : d + 1, at], (ROWS, LANES)) for d in range(3)
                    ]
                    ax = ax + inv3 * (along * dx - tx)
                    ay = ay + inv3 * (along * dy - ty)
                    az = az + inv3 * (along * dz - tz)
                return ax, ay, az

            sums = (acc[0, rows, :], acc[1, rows, :], acc[2, rows, :])
            step = 8
            total = block // (LANES * step)
            if total == 1:
                sums = chunks(0, step, sums)
            else:
                sums = lax.fori_loop(
                    0, total, lambda i, s: chunks(pl.multiple_of(i * step * LANES, LANES), step, s), sums
                )
            acc[0, rows, :], acc[1, rows, :], acc[2, rows, :] = sums

    sweep(pack)

    @pl.loop(1, nc)
    def _(k):
        copy1(k).wait_recv()
        sweep(gath.at[k])

    gain = su[0:1, own]
    c_own = cvol[0:1, own]
    me = c_me * ns + s_me
    new = [gain * (i + 3.0 * lane_sums(acc[d])[0:1]) for d, i in enumerate((ix, iy, iz))]
    scaled = [3.0 * c_own * u for u in new]
    for d in range(3):
        mag[me, d : d + 1, :] = scaled[d]
    mag[me, 3:4, :] = c_own * (new[0] * ix + new[1] * iy + new[2] * iz)
    here = [cp[d : d + 1, own] for d in range(3)]
    mag[me, 4:5, :] = scaled[0] * here[0] + scaled[1] * here[1] + scaled[2] * here[2]

    def copy2(c_who, s_who, slot, k):
        return pltpu.make_async_remote_copy(
            src_ref=mag.at[me], dst_ref=mag.at[slot], send_sem=send2.at[k], recv_sem=recv2.at[slot],
            device_id={"cell": c_who, "stn": s_who}, device_id_type=MESH,
        )

    s_others = [partner(s_me, ks, ns) for ks in range(ns)]
    for ks in range(1, ns):
        copy2(c_me, s_others[ks], me, ks).start()

    @pl.loop(1, nc)
    def _(kc):
        c_who = partner(c_me, kc, nc)
        for ks in range(ns):
            copy2(c_who, s_others[ks], me, kc * ns + ks).start()

    for d in range(3):
        upd[d : d + 1, :] = new[d]

    slots = geo.shape[0] // 2
    chunks_in = block // LANES
    part = min(8, chunks_in)

    def spread(row):
        return jnp.broadcast_to(row, (ROWS, LANES))

    def over_pairs(body):
        @pl.loop(0, share // ROWS)
        def _(g):
            rows = pl.ds(pl.multiple_of(g * ROWS, ROWS), ROWS)
            for p in range(chunks_in // part):
                body(rows, range(p * part, (p + 1) * part))

    def geometry(kc, slot):
        def body(rows, run):
            px, py, pz, pi = stb[0, rows, :], stb[1, rows, :], stb[2, rows, :], stb[3, rows, :]
            for j in run:
                at = slice(j * LANES, (j + 1) * LANES)
                dx, dy, dz = [p - spread(gath[kc, d : d + 1, at]) for d, p in enumerate((px, py, pz))]
                inv = lax.rsqrt(dx * dx + dy * dy + dz * dz + spread(gath[kc, 6:7, at]))
                inv2 = inv * inv
                inv3 = inv2 * inv
                geo[2 * slot, rows, at] = inv3
                geo[2 * slot + 1, rows, at] = (pi - spread(gath[kc, 7:8, at])) * inv2 * inv3

        over_pairs(body)

    def predict(c_who, slot):
        def body(rows, run):
            px, py, pz = stb[0, rows, :], stb[1, rows, :], stb[2, rows, :]
            total = racc[rows, :]
            for j in run:
                at = slice(j * LANES, (j + 1) * LANES)
                start = j * LANES % owned
                who = c_who * ns + j * LANES // owned

                def row(r):
                    return spread(mag[who, r : r + 1, start : start + LANES])

                along = px * row(0) + py * row(1) + pz * row(2) - row(4)
                total = total + (along * geo[2 * slot + 1, rows, at] - row(3) * geo[2 * slot, rows, at])
            racc[rows, :] = total

        over_pairs(body)

    if slots > 1:

        @pl.loop(0, nc)
        def _(kc):
            geometry(kc, kc)

    for t in range(ns):

        @pl.when(s_me != t)
        def _():
            slot = c_me * ns + t
            copy2(c_me, t, slot, 0).wait_recv()

    if slots == 1:
        geometry(0, 0)
    predict(c_me, 0)

    @pl.loop(1, nc)
    def _(kc):
        c_who = partner(c_me, kc, nc)
        for t in range(ns):
            copy2(c_who, t, c_who * ns + t, 0).wait_recv()
        if slots == 1:
            geometry(kc, 0)
            predict(c_who, 0)
        else:
            predict(c_who, kc)

    pred[...] = lane_sums(racc[...])[0:1]

    @pl.loop(1, nc)
    def _(k):
        copy1(k).wait_send()

    @pl.loop(1, nc * ns)
    def _(k):
        copy2(c_me, s_me, me, k).wait_send()


def finish(updated, predictions, updated_out, predictions_out, done):
    moves = [
        pltpu.make_async_copy(updated, updated_out, done.at[0]),
        pltpu.make_async_copy(predictions, predictions_out, done.at[1]),
    ]
    for move in moves:
        move.start()
    for move in moves:
        move.wait()


def shards(cell_points, magnetization, cell_level, suscept, inducing, stations):
    nc = lax.axis_size("cell")
    ns = lax.axis_size("stn")
    block = cell_points.shape[1]
    owned = block // ns
    targets = stations.shape[1]
    share = targets // nc
    slots = nc if nc * share * block * 8 <= 1 << 24 else 1
    f32 = jnp.float32
    vmem = pl.BlockSpec(memory_space=pltpu.VMEM)
    hbm = pl.BlockSpec(memory_space=pltpu.HBM)
    dma = pltpu.SemaphoreType.DMA
    updated, predictions = pl.pallas_call(
        functools.partial(kernel, nc, ns),
        out_shape=(jax.ShapeDtypeStruct((3, owned), f32), jax.ShapeDtypeStruct((1, share), f32)),
        in_specs=[hbm] * 6,
        out_specs=(vmem, vmem),
        scratch_shapes=[
            pltpu.VMEM((3, block), f32),
            pltpu.VMEM((3, block), f32),
            pltpu.VMEM((1, block), jnp.int32),
            pltpu.VMEM((1, block), f32),
            pltpu.SMEM((3,), f32),
            pltpu.VMEM((3, targets), f32),
            pltpu.VMEM((1, block), f32),
            pltpu.VMEM((nc, 8, block), f32),
            pltpu.VMEM((3, owned, LANES), f32),
            pltpu.VMEM((3, owned, LANES), f32),
            pltpu.VMEM((nc * ns, 8, owned), f32),
            pltpu.VMEM((4, share, LANES), f32),
            pltpu.VMEM((share, LANES), f32),
            pltpu.VMEM((2 * slots, share, block), f32),
            pltpu.VMEM((3, block), f32),
            dma((nc,)),
            dma((nc,)),
            dma((nc * ns,)),
            dma((nc * ns,)),
            dma((6,)),
        ],
        compiler_params=pltpu.CompilerParams(
            collective_id=0, has_side_effects=True, vmem_limit_bytes=60 * 1024 * 1024
        ),
    )(
        cell_points,
        magnetization,
        cell_level.reshape(1, block),
        suscept.reshape(1, block),
        inducing,
        stations,
    )
    anywhere = pl.BlockSpec(memory_space=pl.ANY)
    updated, predictions = pl.pallas_call(
        finish,
        out_shape=(jax.ShapeDtypeStruct((3, owned), f32), jax.ShapeDtypeStruct((1, share), f32)),
        in_specs=[anywhere, anywhere],
        out_specs=(anywhere, anywhere),
        scratch_shapes=[dma((2,))],
    )(updated, predictions)
    return updated, predictions.reshape(share)


def solution(mesh):
    placed = (P(None, "cell"), P(None, "cell"), P("cell"), P("cell"), P(), P(None, "stn"))
    return jax.shard_map(
        shards,
        mesh=mesh,
        in_specs=placed,
        out_specs=(P(None, ("cell", "stn")), P(("stn", "cell"))),
        check_vma=False,
    )
```

```python
import functools
import math

import jax
import jax.numpy as jnp
from jax import lax
from jax.experimental import pallas as pl
from jax.experimental.pallas import tpu as pltpu
from jax.sharding import PartitionSpec as P

INV_FOUR_PI = 0.25 / math.pi
MESH = pl.DeviceIdType.MESH
LANES = 128
ROWS = 32


def partner(me, k, n):
    out, bit = 0, 1
    while bit < n:
        out = out + bit * (((me // bit) % 2 + (k // bit) % 2) % 2)
        bit *= 2
    return out


def lane_sums(values):
    ones = jnp.ones((8, LANES), jnp.float32)
    return lax.dot_general(
        ones,
        values,
        (((1,), (1,)), ((), ())),
        precision=lax.Precision.HIGHEST,
        preferred_element_type=jnp.float32,
    )


def kernel(
    nc, ns, cp_hbm, mg_hbm, lv_hbm, su_hbm, ind_hbm, st_hbm, upd, pred,
    cp, mg, lv, su, ind, st, cvol, gath, tgt, acc, mag, stb, racc, geo, third,
    send1, recv1, send2, recv2, loaded,
):
    loads = [
        pltpu.make_async_copy(src, dst, loaded.at[i])
        for i, (src, dst) in enumerate(
            ((lv_hbm, lv), (mg_hbm, mg), (cp_hbm, cp), (ind_hbm, ind), (st_hbm, st), (su_hbm, su))
        )
    ]
    for load in loads:
        load.start()
    block = cp.shape[1]
    owned = block // ns
    share = st.shape[1] // nc
    spacing = float(block * nc) ** (-1.0 / 3.0)
    c_me = lax.axis_index("cell")
    s_me = lax.axis_index("stn")

    barrier = pltpu.get_barrier_semaphore()

    @pl.loop(1, nc)
    def _(k):
        pl.semaphore_signal(barrier, inc=1, device_id={"cell": partner(c_me, k, nc)}, device_id_type=MESH)

    @pl.loop(1, ns)
    def _(k):
        pl.semaphore_signal(barrier, inc=1, device_id={"stn": partner(s_me, k, ns)}, device_id_type=MESH)

    for load in loads[:4]:
        load.wait()
    ix, iy, iz = ind[0], ind[1], ind[2]
    level = lv[...]
    size_h = spacing * jnp.where(level == 0, 1.0, jnp.where(level == 1, 0.5, 0.25))
    strength = INV_FOUR_PI * size_h * size_h * size_h
    pack = gath.at[0]
    pack[0:3, :] = cp[...]
    pack[3:6, :] = mg[...] * strength
    pack[6:7, :] = size_h * size_h
    pack[7:8, :] = cp[0:1, :] * ix + cp[1:2, :] * iy + cp[2:3, :] * iz
    cvol[...] = strength

    pl.semaphore_wait(barrier, nc - 1 + ns - 1)

    def copy1(k):
        return pltpu.make_async_remote_copy(
            src_ref=gath.at[0], dst_ref=gath.at[k], send_sem=send1.at[k], recv_sem=recv1.at[k],
            device_id={"cell": partner(c_me, k, nc)}, device_id_type=MESH,
        )

    @pl.loop(1, nc)
    def _(k):
        copy1(k).start()

    offset = s_me * owned
    own = pl.ds(pl.multiple_of(offset, LANES), owned)
    for d in range(3):
        for t in range(owned // LANES):
            row = cp[d : d + 1, pl.ds(pl.multiple_of(offset + t * LANES, LANES), LANES)]
            tgt[d, t * LANES : (t + 1) * LANES, :] = jnp.broadcast_to(row, (LANES, LANES)).T
    acc[...] = jnp.zeros_like(acc)

    for load in loads[4:]:
        load.wait()
    mine = pl.ds(pl.multiple_of(c_me * share, LANES), share)
    place = [jnp.broadcast_to(st[d : d + 1, mine], (LANES, share)).T for d in range(3)]
    for d in range(3):
        stb[d] = place[d]
    stb[3] = place[0] * ix + place[1] * iy + place[2] * iz
    racc[...] = jnp.zeros_like(racc)

    def sweep(src):
        third[...] = src[3:6, :] * (1.0 / 3.0)

        @pl.loop(0, owned // ROWS)
        def _(g):
            rows = pl.ds(pl.multiple_of(g * ROWS, ROWS), ROWS)
            px, py, pz = tgt[0, rows, :], tgt[1, rows, :], tgt[2, rows, :]

            def chunks(start, count, sums):
                ax, ay, az = sums
                for j in range(count):
                    at = pl.ds(start + j * LANES, LANES)

                    def row(r):
                        return jnp.broadcast_to(src[r : r + 1, at], (ROWS, LANES))

                    dx, dy, dz = px - row(0), py - row(1), pz - row(2)
                    mx, my, mz = row(3), row(4), row(5)
                    inv = lax.rsqrt(dx * dx + dy * dy + dz * dz + row(6))
                    inv2 = inv * inv
                    inv3 = inv2 * inv
                    along = (dx * mx + dy * my + dz * mz) * inv2
                    tx, ty, tz = [
                        jnp.broadcast_to(third[d : d + 1, at], (ROWS, LANES)) for d in range(3)
                    ]
                    ax = ax + inv3 * (along * dx - tx)
                    ay = ay + inv3 * (along * dy - ty)
                    az = az + inv3 * (along * dz - tz)
                return ax, ay, az

            sums = (acc[0, rows, :], acc[1, rows, :], acc[2, rows, :])
            step = 8
            total = block // (LANES * step)
            if total == 1:
                sums = chunks(0, step, sums)
            else:
                sums = lax.fori_loop(
                    0, total, lambda i, s: chunks(pl.multiple_of(i * step * LANES, LANES), step, s), sums
                )
            acc[0, rows, :], acc[1, rows, :], acc[2, rows, :] = sums

    sweep(pack)

    @pl.loop(1, nc)
    def _(k):
        copy1(k).wait_recv()
        sweep(gath.at[k])

    gain = su[0:1, own]
    c_own = cvol[0:1, own]
    me = c_me * ns + s_me
    new = [gain * (i + 3.0 * lane_sums(acc[d])[0:1]) for d, i in enumerate((ix, iy, iz))]
    scaled = [3.0 * c_own * u for u in new]
    for d in range(3):
        mag[me, d : d + 1, :] = scaled[d]
    mag[me, 3:4, :] = c_own * (new[0] * ix + new[1] * iy + new[2] * iz)
    here = [cp[d : d + 1, own] for d in range(3)]
    mag[me, 4:5, :] = scaled[0] * here[0] + scaled[1] * here[1] + scaled[2] * here[2]

    def copy2(c_who, s_who, kc):
        return pltpu.make_async_remote_copy(
            src_ref=mag.at[me], dst_ref=mag.at[me], send_sem=send2.at[0], recv_sem=recv2.at[kc],
            device_id={"cell": c_who, "stn": s_who}, device_id_type=MESH,
        )

    s_others = [partner(s_me, ks, ns) for ks in range(ns)]
    for ks in range(1, ns):
        copy2(c_me, s_others[ks], 0).start()

    @pl.loop(1, nc)
    def _(kc):
        c_who = partner(c_me, kc, nc)
        for ks in range(ns):
            copy2(c_who, s_others[ks], kc).start()

    for d in range(3):
        upd[d : d + 1, :] = new[d]

    slots = geo.shape[0] // 2
    chunks_in = block // LANES
    part = min(8, chunks_in)

    def spread(row):
        return jnp.broadcast_to(row, (ROWS, LANES))

    def over_pairs(body):
        @pl.loop(0, share // ROWS)
        def _(g):
            rows = pl.ds(pl.multiple_of(g * ROWS, ROWS), ROWS)
            for p in range(chunks_in // part):
                body(rows, range(p * part, (p + 1) * part))

    def geometry(kc, slot):
        def body(rows, run):
            px, py, pz, pi = stb[0, rows, :], stb[1, rows, :], stb[2, rows, :], stb[3, rows, :]
            for j in run:
                at = slice(j * LANES, (j + 1) * LANES)
                dx, dy, dz = [p - spread(gath[kc, d : d + 1, at]) for d, p in enumerate((px, py, pz))]
                inv = lax.rsqrt(dx * dx + dy * dy + dz * dz + spread(gath[kc, 6:7, at]))
                inv2 = inv * inv
                inv3 = inv2 * inv
                geo[2 * slot, rows, at] = inv3
                geo[2 * slot + 1, rows, at] = (pi - spread(gath[kc, 7:8, at])) * inv2 * inv3

        over_pairs(body)

    def predict(c_who, slot):
        def body(rows, run):
            px, py, pz = stb[0, rows, :], stb[1, rows, :], stb[2, rows, :]
            total = racc[rows, :]
            for j in run:
                at = slice(j * LANES, (j + 1) * LANES)
                start = j * LANES % owned
                who = c_who * ns + j * LANES // owned

                def row(r):
                    return spread(mag[who, r : r + 1, start : start + LANES])

                along = px * row(0) + py * row(1) + pz * row(2) - row(4)
                total = total + (along * geo[2 * slot + 1, rows, at] - row(3) * geo[2 * slot, rows, at])
            racc[rows, :] = total

        over_pairs(body)

    if slots > 1:

        @pl.loop(0, nc)
        def _(kc):
            geometry(kc, kc)

    def wait_pieces(sem, count):
        held = mag.at[pl.ds(0, count)]
        pltpu.make_async_copy(held, held, sem).wait()

    wait_pieces(recv2.at[0], ns - 1)
    if slots == 1:
        geometry(0, 0)
    predict(c_me, 0)

    @pl.loop(1, nc)
    def _(kc):
        c_who = partner(c_me, kc, nc)
        wait_pieces(recv2.at[kc], ns)
        if slots == 1:
            geometry(kc, 0)
            predict(c_who, 0)
        else:
            predict(c_who, kc)

    pred[...] = lane_sums(racc[...])[0:1]

    @pl.loop(1, nc)
    def _(k):
        copy1(k).wait_send()

    wait_pieces(send2.at[0], nc * ns - 1)


def finish(updated, predictions, updated_out, predictions_out, done):
    moves = [
        pltpu.make_async_copy(updated, updated_out, done.at[0]),
        pltpu.make_async_copy(predictions, predictions_out, done.at[1]),
    ]
    for move in moves:
        move.start()
    for move in moves:
        move.wait()


def shards(cell_points, magnetization, cell_level, suscept, inducing, stations):
    nc = lax.axis_size("cell")
    ns = lax.axis_size("stn")
    block = cell_points.shape[1]
    owned = block // ns
    targets = stations.shape[1]
    share = targets // nc
    slots = nc if nc * share * block * 8 <= 1 << 24 else 1
    f32 = jnp.float32
    vmem = pl.BlockSpec(memory_space=pltpu.VMEM)
    hbm = pl.BlockSpec(memory_space=pltpu.HBM)
    dma = pltpu.SemaphoreType.DMA
    updated, predictions = pl.pallas_call(
        functools.partial(kernel, nc, ns),
        out_shape=(jax.ShapeDtypeStruct((3, owned), f32), jax.ShapeDtypeStruct((1, share), f32)),
        in_specs=[hbm] * 6,
        out_specs=(vmem, vmem),
        scratch_shapes=[
            pltpu.VMEM((3, block), f32),
            pltpu.VMEM((3, block), f32),
            pltpu.VMEM((1, block), jnp.int32),
            pltpu.VMEM((1, block), f32),
            pltpu.SMEM((3,), f32),
            pltpu.VMEM((3, targets), f32),
            pltpu.VMEM((1, block), f32),
            pltpu.VMEM((nc, 8, block), f32),
            pltpu.VMEM((3, owned, LANES), f32),
            pltpu.VMEM((3, owned, LANES), f32),
            pltpu.VMEM((nc * ns, 8, owned), f32),
            pltpu.VMEM((4, share, LANES), f32),
            pltpu.VMEM((share, LANES), f32),
            pltpu.VMEM((2 * slots, share, block), f32),
            pltpu.VMEM((3, block), f32),
            dma((nc,)),
            dma((nc,)),
            dma((1,)),
            dma((nc,)),
            dma((6,)),
        ],
        compiler_params=pltpu.CompilerParams(
            collective_id=0, has_side_effects=True, vmem_limit_bytes=60 * 1024 * 1024
        ),
    )(
        cell_points,
        magnetization,
        cell_level.reshape(1, block),
        suscept.reshape(1, block),
        inducing,
        stations,
    )
    anywhere = pl.BlockSpec(memory_space=pl.ANY)
    updated, predictions = pl.pallas_call(
        finish,
        out_shape=(jax.ShapeDtypeStruct((3, owned), f32), jax.ShapeDtypeStruct((1, share), f32)),
        in_specs=[anywhere, anywhere],
        out_specs=(anywhere, anywhere),
        scratch_shapes=[dma((2,))],
    )(updated, predictions)
    return updated, predictions.reshape(share)


def solution(mesh):
    placed = (P(None, "cell"), P(None, "cell"), P("cell"), P("cell"), P(), P(None, "stn"))
    return jax.shard_map(
        shards,
        mesh=mesh,
        in_specs=placed,
        out_specs=(P(None, ("cell", "stn")), P(("stn", "cell"))),
        check_vma=False,
    )
```

```python
import functools
import math

import jax
import jax.numpy as jnp
from jax import lax
from jax.experimental import pallas as pl
from jax.experimental.pallas import tpu as pltpu
from jax.sharding import PartitionSpec as P

INV_FOUR_PI = 0.25 / math.pi
MESH = pl.DeviceIdType.MESH
LANES = 128
ROWS = 32


def partner(me, k, n):
    out, bit = 0, 1
    while bit < n:
        out = out + bit * (((me // bit) % 2 + (k // bit) % 2) % 2)
        bit *= 2
    return out


def lane_sums(values):
    ones = jnp.ones((8, LANES), jnp.float32)
    return lax.dot_general(
        ones,
        values,
        (((1,), (1,)), ((), ())),
        precision=lax.Precision.HIGHEST,
        preferred_element_type=jnp.float32,
    )


def kernel(
    nc, ns, cp_hbm, mg_hbm, lv_hbm, su_hbm, ind_hbm, st_hbm, upd, pred,
    cp, mg, lv, su, ind, st, cvol, gath, tgt, acc, mag, stb, racc, geo, third,
    send1, recv1, send2, recv2, loaded,
):
    loads = [
        pltpu.make_async_copy(src, dst, loaded.at[i])
        for i, (src, dst) in enumerate(
            ((lv_hbm, lv), (mg_hbm, mg), (cp_hbm, cp), (ind_hbm, ind), (st_hbm, st), (su_hbm, su))
        )
    ]
    for load in loads:
        load.start()
    block = cp.shape[1]
    owned = block // ns
    share = st.shape[1] // nc
    spacing = float(block * nc) ** (-1.0 / 3.0)
    c_me = lax.axis_index("cell")
    s_me = lax.axis_index("stn")

    barrier = pltpu.get_barrier_semaphore()

    @pl.loop(1, nc)
    def _(k):
        pl.semaphore_signal(barrier, inc=1, device_id={"cell": partner(c_me, k, nc)}, device_id_type=MESH)

    @pl.loop(1, ns)
    def _(k):
        pl.semaphore_signal(barrier, inc=1, device_id={"stn": partner(s_me, k, ns)}, device_id_type=MESH)

    for load in loads[:4]:
        load.wait()
    ix, iy, iz = ind[0], ind[1], ind[2]
    level = lv[...]
    size_h = spacing * jnp.where(level == 0, 1.0, jnp.where(level == 1, 0.5, 0.25))
    strength = INV_FOUR_PI * size_h * size_h * size_h
    pack = gath.at[0]
    pack[0:3, :] = cp[...]
    pack[3:6, :] = mg[...] * strength
    pack[6:7, :] = size_h * size_h
    pack[7:8, :] = cp[0:1, :] * ix + cp[1:2, :] * iy + cp[2:3, :] * iz
    cvol[...] = strength

    pl.semaphore_wait(barrier, nc - 1 + ns - 1)

    def copy1(k):
        return pltpu.make_async_remote_copy(
            src_ref=gath.at[0], dst_ref=gath.at[k], send_sem=send1.at[k], recv_sem=recv1.at[k],
            device_id={"cell": partner(c_me, k, nc)}, device_id_type=MESH,
        )

    @pl.loop(1, nc)
    def _(k):
        copy1(k).start()

    offset = s_me * owned
    own = pl.ds(pl.multiple_of(offset, LANES), owned)
    for d in range(3):
        for t in range(owned // LANES):
            row = cp[d : d + 1, pl.ds(pl.multiple_of(offset + t * LANES, LANES), LANES)]
            tgt[d, t * LANES : (t + 1) * LANES, :] = jnp.broadcast_to(row, (LANES, LANES)).T
    acc[...] = jnp.zeros_like(acc)

    def sweep(src):
        third[...] = src[3:6, :] * (1.0 / 3.0)

        @pl.loop(0, owned // ROWS)
        def _(g):
            rows = pl.ds(pl.multiple_of(g * ROWS, ROWS), ROWS)
            px, py, pz = tgt[0, rows, :], tgt[1, rows, :], tgt[2, rows, :]

            def chunks(start, count, sums):
                ax, ay, az = sums
                for j in range(count):
                    at = pl.ds(start + j * LANES, LANES)

                    def row(r):
                        return jnp.broadcast_to(src[r : r + 1, at], (ROWS, LANES))

                    dx, dy, dz = px - row(0), py - row(1), pz - row(2)
                    mx, my, mz = row(3), row(4), row(5)
                    inv = lax.rsqrt(dx * dx + dy * dy + dz * dz + row(6))
                    inv2 = inv * inv
                    inv3 = inv2 * inv
                    along = (dx * mx + dy * my + dz * mz) * inv2
                    tx, ty, tz = [
                        jnp.broadcast_to(third[d : d + 1, at], (ROWS, LANES)) for d in range(3)
                    ]
                    ax = ax + inv3 * (along * dx - tx)
                    ay = ay + inv3 * (along * dy - ty)
                    az = az + inv3 * (along * dz - tz)
                return ax, ay, az

            sums = (acc[0, rows, :], acc[1, rows, :], acc[2, rows, :])
            step = 8
            total = block // (LANES * step)
            if total == 1:
                sums = chunks(0, step, sums)
            else:
                sums = lax.fori_loop(
                    0, total, lambda i, s: chunks(pl.multiple_of(i * step * LANES, LANES), step, s), sums
                )
            acc[0, rows, :], acc[1, rows, :], acc[2, rows, :] = sums

    sweep(pack)

    @pl.loop(1, nc)
    def _(k):
        copy1(k).wait_recv()
        sweep(gath.at[k])

    for load in loads[4:]:
        load.wait()
    gain = su[0:1, own]
    c_own = cvol[0:1, own]
    me = c_me * ns + s_me
    new = [gain * (i + 3.0 * lane_sums(acc[d])[0:1]) for d, i in enumerate((ix, iy, iz))]
    scaled = [3.0 * c_own * u for u in new]
    for d in range(3):
        mag[me, d : d + 1, :] = scaled[d]
    mag[me, 3:4, :] = c_own * (new[0] * ix + new[1] * iy + new[2] * iz)
    here = [cp[d : d + 1, own] for d in range(3)]
    mag[me, 4:5, :] = scaled[0] * here[0] + scaled[1] * here[1] + scaled[2] * here[2]

    def copy2(c_who, s_who, kc):
        return pltpu.make_async_remote_copy(
            src_ref=mag.at[me], dst_ref=mag.at[me], send_sem=send2.at[0], recv_sem=recv2.at[kc],
            device_id={"cell": c_who, "stn": s_who}, device_id_type=MESH,
        )

    s_others = [partner(s_me, ks, ns) for ks in range(ns)]
    for ks in range(1, ns):
        copy2(c_me, s_others[ks], 0).start()

    @pl.loop(1, nc)
    def _(kc):
        c_who = partner(c_me, kc, nc)
        for ks in range(ns):
            copy2(c_who, s_others[ks], kc).start()

    for d in range(3):
        upd[d : d + 1, :] = new[d]

    mine = pl.ds(pl.multiple_of(c_me * share, LANES), share)
    place = [jnp.broadcast_to(st[d : d + 1, mine], (LANES, share)).T for d in range(3)]
    for d in range(3):
        stb[d] = place[d]
    stb[3] = place[0] * ix + place[1] * iy + place[2] * iz
    racc[...] = jnp.zeros_like(racc)

    slots = geo.shape[0] // 2
    chunks_in = block // LANES
    part = min(8, chunks_in)

    def spread(row):
        return jnp.broadcast_to(row, (ROWS, LANES))

    def over_pairs(body):
        @pl.loop(0, share // ROWS)
        def _(g):
            rows = pl.ds(pl.multiple_of(g * ROWS, ROWS), ROWS)
            for p in range(chunks_in // part):
                body(rows, range(p * part, (p + 1) * part))

    def geometry(kc, slot):
        def body(rows, run):
            px, py, pz, pi = stb[0, rows, :], stb[1, rows, :], stb[2, rows, :], stb[3, rows, :]
            for j in run:
                at = slice(j * LANES, (j + 1) * LANES)
                dx, dy, dz = [p - spread(gath[kc, d : d + 1, at]) for d, p in enumerate((px, py, pz))]
                inv = lax.rsqrt(dx * dx + dy * dy + dz * dz + spread(gath[kc, 6:7, at]))
                inv2 = inv * inv
                inv3 = inv2 * inv
                geo[2 * slot, rows, at] = inv3
                geo[2 * slot + 1, rows, at] = (pi - spread(gath[kc, 7:8, at])) * inv2 * inv3

        over_pairs(body)

    def predict(c_who, slot):
        def body(rows, run):
            px, py, pz = stb[0, rows, :], stb[1, rows, :], stb[2, rows, :]
            total = racc[rows, :]
            for j in run:
                at = slice(j * LANES, (j + 1) * LANES)
                start = j * LANES % owned
                who = c_who * ns + j * LANES // owned

                def row(r):
                    return spread(mag[who, r : r + 1, start : start + LANES])

                along = px * row(0) + py * row(1) + pz * row(2) - row(4)
                total = total + (along * geo[2 * slot + 1, rows, at] - row(3) * geo[2 * slot, rows, at])
            racc[rows, :] = total

        over_pairs(body)

    if slots > 1:

        @pl.loop(0, nc)
        def _(kc):
            geometry(kc, kc)

    def wait_pieces(sem, count):
        held = mag.at[pl.ds(0, count)]
        pltpu.make_async_copy(held, held, sem).wait()

    wait_pieces(recv2.at[0], ns - 1)
    if slots == 1:
        geometry(0, 0)
    predict(c_me, 0)

    @pl.loop(1, nc)
    def _(kc):
        c_who = partner(c_me, kc, nc)
        wait_pieces(recv2.at[kc], ns)
        if slots == 1:
            geometry(kc, 0)
            predict(c_who, 0)
        else:
            predict(c_who, kc)

    pred[...] = lane_sums(racc[...])[0:1]

    @pl.loop(1, nc)
    def _(k):
        copy1(k).wait_send()

    wait_pieces(send2.at[0], nc * ns - 1)


def finish(updated, predictions, updated_out, predictions_out, done):
    moves = [
        pltpu.make_async_copy(updated, updated_out, done.at[0]),
        pltpu.make_async_copy(predictions, predictions_out, done.at[1]),
    ]
    for move in moves:
        move.start()
    for move in moves:
        move.wait()


def shards(cell_points, magnetization, cell_level, suscept, inducing, stations):
    nc = lax.axis_size("cell")
    ns = lax.axis_size("stn")
    block = cell_points.shape[1]
    owned = block // ns
    targets = stations.shape[1]
    share = targets // nc
    slots = nc if nc * share * block * 8 <= 1 << 24 else 1
    f32 = jnp.float32
    vmem = pl.BlockSpec(memory_space=pltpu.VMEM)
    hbm = pl.BlockSpec(memory_space=pltpu.HBM)
    dma = pltpu.SemaphoreType.DMA
    updated, predictions = pl.pallas_call(
        functools.partial(kernel, nc, ns),
        out_shape=(jax.ShapeDtypeStruct((3, owned), f32), jax.ShapeDtypeStruct((1, share), f32)),
        in_specs=[hbm] * 6,
        out_specs=(vmem, vmem),
        scratch_shapes=[
            pltpu.VMEM((3, block), f32),
            pltpu.VMEM((3, block), f32),
            pltpu.VMEM((1, block), jnp.int32),
            pltpu.VMEM((1, block), f32),
            pltpu.SMEM((3,), f32),
            pltpu.VMEM((3, targets), f32),
            pltpu.VMEM((1, block), f32),
            pltpu.VMEM((nc, 8, block), f32),
            pltpu.VMEM((3, owned, LANES), f32),
            pltpu.VMEM((3, owned, LANES), f32),
            pltpu.VMEM((nc * ns, 8, owned), f32),
            pltpu.VMEM((4, share, LANES), f32),
            pltpu.VMEM((share, LANES), f32),
            pltpu.VMEM((2 * slots, share, block), f32),
            pltpu.VMEM((3, block), f32),
            dma((nc,)),
            dma((nc,)),
            dma((1,)),
            dma((nc,)),
            dma((6,)),
        ],
        compiler_params=pltpu.CompilerParams(
            collective_id=0, has_side_effects=True, vmem_limit_bytes=60 * 1024 * 1024
        ),
    )(
        cell_points,
        magnetization,
        cell_level.reshape(1, block),
        suscept.reshape(1, block),
        inducing,
        stations,
    )
    anywhere = pl.BlockSpec(memory_space=pl.ANY)
    updated, predictions = pl.pallas_call(
        finish,
        out_shape=(jax.ShapeDtypeStruct((3, owned), f32), jax.ShapeDtypeStruct((1, share), f32)),
        in_specs=[anywhere, anywhere],
        out_specs=(anywhere, anywhere),
        scratch_shapes=[dma((2,))],
    )(updated, predictions)
    return updated, predictions.reshape(share)


def solution(mesh):
    placed = (P(None, "cell"), P(None, "cell"), P("cell"), P("cell"), P(), P(None, "stn"))
    return jax.shard_map(
        shards,
        mesh=mesh,
        in_specs=placed,
        out_specs=(P(None, ("cell", "stn")), P(("stn", "cell"))),
        check_vma=False,
    )
```
